32 devices in a mesh: ctx: 16 (over z, y, x), head: 2 (over core).
Axes of the slice: x: 2, y: 2, z: 4, core: 2. Of those that a mesh axis runs over, the one named last changes fastest.
Arguments:
- queries: bfloat16 [1024, 16, 576], P('ctx', 'head'), may hold values from -48 to 48
- latent: bfloat16 [1024, 576], P('ctx'), may hold values from -9 to 9
- w_uv: bfloat16 [16, 512, 128], P('head'), may hold values from -0.25 to 0.25
- w_out: bfloat16 [2048, 3584], P('ctx', 'head'), may hold values from -0.125 to 0.125
- pair_perm: int32 [16], replicated, may hold values from 0 to 15, each once
Outputs:
- mixed: bfloat16 [1024, 3584], P('ctx', 'head')
The draws below stay inside these ranges and needn't reach their ends.
Inputs may be any that keep to these rules, and one draw needn't show every extreme that they name: `pair_perm`: a permutation of the span pairs.
All inputs are finite; a program needn't handle non-finite values.
Results may differ from the reference program's by a relative error of at most 0.0075.
Values may be sent and summed in bfloat16 or wider, within the bound.
A program may use at most 64 MiB of HBM per device.

```python
import jax
import jax.numpy as jnp
from jax import lax

HEADS = 16
LAT = 512
QKW = 576
VDIM = 128
DOUT = 3584
TOK_DEV = 64
TOKENS = 1024
N_CTX = 16


def latent_values(key):
    normal_part = jnp.clip(jax.random.normal(key, (TOKENS, QKW), jnp.float32), -4.0, 4.0)
    return normal_part


def draw_latent(key, part):
    rows_drawn = latent_values(key)
    return rows_drawn.astype(jnp.bfloat16)


def draw_queries(key, part):
    key = jax.random.fold_in(key, 5)
    query_vals = jnp.clip(jax.random.normal(key, (TOKENS, HEADS, QKW), jnp.float32), -4.0, 4.0)
    return query_vals.astype(jnp.bfloat16)


def levels(own_key, shape, pieces, low, largest):
    gain = 1.0
    for position, blocks in pieces:
        steps = jax.random.uniform(jax.random.fold_in(jax.random.fold_in(own_key, 6), position), (blocks,), jnp.float32, low / len(pieces), largest / len(pieces))
        gain = gain * jnp.repeat(jnp.exp(steps), shape[position] // blocks).reshape((-1,) + (1,) * (len(shape) - 1 - position))
    return gain


def centred(stream_key, extent, width, most, pieces=(), kind=jnp.bfloat16):
    result = jax.random.normal(stream_key, extent, jnp.float32) * width
    if len(pieces) > 0:
        result = levels(stream_key, extent, pieces, -0.22, 0.18) * result
    return jnp.clip(result, min=-most, max=most).astype(kind)


def setup_inputs(seed: int = 0) -> dict:
    arg_keys = jax.random.split(jax.random.key(seed), 6)
    return {
        "queries": draw_queries(jax.random.fold_in(arg_keys[5], 71), 0),
        "latent": draw_latent(jax.random.fold_in(arg_keys[5], 71), 0),
        "w_uv": centred(arg_keys[2], (HEADS, LAT, VDIM), LAT ** -0.5, 0.25, ((0, 2),)),
        "w_out": centred(arg_keys[3], (HEADS * VDIM, DOUT), (HEADS * VDIM) ** -0.5, 0.125, ((0, 16), (1, 2))),
        "pair_perm": jax.random.permutation(arg_keys[4], N_CTX).astype(jnp.int32),
    }


score_scale = 192.0 ** -0.5


def positions(pair_perm, tok_dev):
    ctx_size = pair_perm.shape[0]
    span_len = tok_dev // 2
    row_ids = jnp.arange(ctx_size * tok_dev, dtype=jnp.int32)
    holder = row_ids // tok_dev
    within = row_ids % tok_dev
    pair_ids = pair_perm[holder]
    span_ids = jnp.where(within >= span_len, 2 * ctx_size - 1 - pair_ids, pair_ids)
    return span_ids * span_len + within % span_len


def reference(queries, latent, w_uv, w_out, pair_perm):
    seq_pos = positions(pair_perm, TOK_DEV)
    visible = seq_pos[None, :] <= seq_pos[:, None]
    key_part = latent[:, :LAT]

    def one_head(head_id):
        query_rows = queries[:, head_id, :]
        scores = jnp.dot(query_rows, latent.T, preferred_element_type=jnp.float32) * score_scale
        scores = jnp.where(visible, scores, -1e30)
        ceiling = jnp.max(scores, axis=1, keepdims=True)
        weights = jnp.where(visible, jnp.exp(scores - ceiling), 0.0)
        mass_sum = jnp.sum(weights, axis=1)
        context = jnp.dot(weights.astype(jnp.bfloat16), key_part, preferred_element_type=jnp.float32) / mass_sum[:, None]
        context = context.astype(jnp.bfloat16)
        return jnp.dot(context, w_uv[head_id], preferred_element_type=jnp.float32).astype(jnp.bfloat16)

    per_head = lax.map(one_head, jnp.arange(HEADS, dtype=jnp.int32))
    values = jnp.transpose(per_head, (1, 0, 2)).reshape(TOKENS, HEADS * VDIM)
    return jnp.dot(values, w_out, preferred_element_type=jnp.float32).astype(jnp.bfloat16)
```

```python
import functools

import jax
import jax.numpy as jnp
from jax import lax
from jax.experimental import pallas as pl
from jax.experimental.pallas import tpu as pltpu
from jax.sharding import PartitionSpec as P

LAT = 512
VDIM = 128
MESH = pl.DeviceIdType.MESH

score_scale = 192.0 ** (-0.5)


def split_ctx(n_ctx):
    low = 1
    while low * low < n_ctx:
        low *= 2
    return n_ctx // low, low


def kernel(
    dims,
    perm_ref,
    lat_ref,
    q_hbm,
    uv_hbm,
    w_hbm,
    out_ref,
    q_ref,
    uv_ref,
    lat,
    ctx_f32,
    w1,
    w2,
    vals1,
    vals2,
    x1,
    x2,
    part1,
    part2,
    send1,
    send2,
    got1,
    got2,
    local_sems,
    hi_send,
    hi_recv,
    lo_send,
    lo_recv,
    core_send,
    core_recv,
    w1_send,
    w1_recv,
    w2_send,
    w2_recv,
    v1_send,
    v1_recv,
    v2_send,
    v2_recv,
    r1_send,
    r1_recv,
    r2_send,
    r2_recv,
):
    n_hi, n_lo, n_head, tok, heads, cols1 = dims
    n_ctx = n_hi * n_lo
    ratio = heads // n_lo
    pieces = 2 if n_head == 2 else 1
    rows_piece = tok // pieces
    me = lax.axis_index("ctx")
    k = lax.axis_index("head")
    hi = me // n_lo
    lo = lax.rem(me, n_lo)

    def hi_at(d):
        return lax.rem(hi + (d + n_hi) % n_hi, n_hi)

    def lo_at(d):
        return lax.rem(lo + (d + n_lo) % n_lo, n_lo)

    def k_at(d):
        return lax.rem(k + (d + n_head) % n_head, n_head)

    def device(h, l, kk):
        return (h * n_lo + l, kk)

    def remote(src, dst, send, recv, target):
        return pltpu.make_async_remote_copy(
            src_ref=src,
            dst_ref=dst,
            send_sem=send,
            recv_sem=recv,
            device_id=target,
            device_id_type=MESH,
        )

    q_copy = pltpu.make_async_copy(q_hbm, q_ref, local_sems.at[0])
    uv_copy = pltpu.make_async_copy(uv_hbm, uv_ref, local_sems.at[1])
    w1_copy = pltpu.make_async_copy(
        w_hbm.at[:, pl.ds(0, cols1)],
        w1.at[pl.ds(pl.multiple_of(hi * VDIM, VDIM), VDIM), :],
        local_sems.at[2],
    )
    w2_copy = pltpu.make_async_copy(
        w_hbm.at[:, pl.ds(cols1, w_hbm.shape[1] - cols1)],
        w2.at[pl.ds(pl.multiple_of(lo * VDIM, VDIM), VDIM), :],
        local_sems.at[3],
    )

    partners = [(0, dl, dk) for dl in range(n_lo) for dk in range(n_head) if dl or dk]
    partners += [(dh, 0, dk) for dh in range(1, n_hi) for dk in range(n_head)]
    barrier = pltpu.get_barrier_semaphore()
    for dh, dl, dk in partners:
        pl.semaphore_signal(
            barrier,
            inc=1,
            device_id=device(hi_at(dh), lo_at(dl), k_at(dk)),
            device_id_type=MESH,
        )
    lat[pl.ds(pl.multiple_of(me * tok, tok), tok), :] = lat_ref[...]
    pl.semaphore_wait(barrier, len(partners))

    def piece(dh, dl, kk):
        owner = hi_at(-dh) * n_lo + lo_at(-dl)
        start = owner * tok
        if pieces > 1:
            start = start + kk * rows_piece
        return lat.at[pl.ds(pl.multiple_of(start, rows_piece), rows_piece), :]

    own = piece(0, 0, k)
    sent = []

    def start(copy):
        copy.start()
        sent.append(copy)

    def to_hi(d):
        return remote(own, own, hi_send.at[d], hi_recv.at[d], device(hi_at(d), lo, k))

    def to_lo(dh, d):
        block = piece(dh, 0, k)
        return remote(
            block, block, lo_send.at[dh, d], lo_recv.at[dh, d], device(hi, lo_at(d), k)
        )

    def to_core(dh, dl):
        block = piece(dh, dl, k)
        return remote(
            block, block, core_send.at[dh, dl], core_recv.at[dh, dl], device(hi, lo, k_at(1))
        )

    def arrived(block, recv):
        remote(block, block, recv, recv, device(hi, lo, k_at(1))).wait_recv()

    for d in range(1, n_hi):
        start(to_hi(d))
    for d in range(1, n_lo):
        start(to_lo(0, d))
    for d in range(1, n_lo):
        start(
            remote(
                w_hbm.at[:, pl.ds(cols1, w_hbm.shape[1] - cols1)],
                w2.at[pl.ds(pl.multiple_of(lo * VDIM, VDIM), VDIM), :],
                w2_send.at[d],
                w2_recv.at[d],
                device(hi, lo_at(d), k),
            )
        )
    for d in range(1, n_hi):
        start(
            remote(
                w_hbm.at[:, pl.ds(0, cols1)],
                w1.at[pl.ds(pl.multiple_of(hi * VDIM, VDIM), VDIM), :],
                w1_send.at[d],
                w1_recv.at[d],
                device(hi_at(d), lo, k),
            )
        )
    for copy in (q_copy, uv_copy, w1_copy, w2_copy):
        copy.start()
    for d in range(1, n_hi):
        arrived(piece(d, 0, k), hi_recv.at[d])
        for e in range(1, n_lo):
            start(to_lo(d, e))
        if pieces > 1:
            start(to_core(d, 0))
    for dh in range(n_hi):
        for dl in range(1, n_lo):
            arrived(piece(dh, dl, k), lo_recv.at[dh, dl])
            if pieces > 1:
                start(to_core(dh, dl))

    total = n_ctx * tok
    half = tok // 2
    key_ids = lax.broadcasted_iota(jnp.int32, (1, total), 1)
    holder = key_ids // tok
    pair = jnp.zeros((1, total), jnp.int32)
    for c in range(n_ctx):
        pair = jnp.where(holder == c, perm_ref[c], pair)
    within = lax.rem(key_ids, tok)
    key_pos = jnp.where(within >= half, 2 * n_ctx - 1 - pair, pair) * half + lax.rem(within, half)
    my_pair = perm_ref[me]

    q_copy.wait()
    uv_copy.wait()
    if pieces > 1:
        for dh in range(n_hi):
            for dl in range(n_lo):
                if dh or dl:
                    arrived(piece(dh, dl, k_at(1)), core_recv.at[dh, dl])

    all_rows = tok * heads
    rows = 256 if total <= 1024 else 64
    for first in range(0, all_rows, rows):
        row_tok = (first + lax.broadcasted_iota(jnp.int32, (rows, 1), 0)) // heads
        query_pos = jnp.where(
            row_tok >= half, 2 * n_ctx - 1 - my_pair, my_pair
        ) * half + lax.rem(row_tok, half)
        scores = (
            lax.dot_general(
                q_ref[pl.ds(first, rows), :],
                lat[...],
                (((1,), (1,)), ((), ())),
                preferred_element_type=jnp.float32,
            )
            * score_scale
        )
        scores = jnp.where(key_pos <= query_pos, scores, -1e30)
        weights = jnp.exp(scores - jnp.max(scores, axis=1, keepdims=True))
        mass = jnp.sum(weights, axis=1, keepdims=True)
        numerator = jnp.dot(
            weights.astype(jnp.bfloat16), lat[:, pl.ds(0, LAT)], preferred_element_type=jnp.float32
        )
        context = numerator / mass
        for j in range(LAT // 128):
            ctx_f32[j, pl.ds(first, rows), :] = context[:, j * 128 : (j + 1) * 128]

    for h in range(heads):
        context = jnp.concatenate(
            [ctx_f32[j, pl.ds(h, tok, stride=heads), :] for j in range(LAT // 128)], axis=1
        ).astype(jnp.bfloat16)
        value = jnp.dot(context, uv_ref[h], preferred_element_type=jnp.float32).astype(jnp.bfloat16)
        r, l = h // n_lo, h % n_lo
        vals1[l, :, pl.ds(r * VDIM, VDIM)] = value
        vals2[r, :, pl.ds(l * VDIM, VDIM)] = value

    owner_k = hi // ratio
    mine = k == owner_k

    @pl.when(mine)
    def _():
        x2[hi] = vals2[lax.rem(hi, ratio)]

    def x2_copy(r, dk):
        return remote(
            vals2.at[r],
            x2.at[hi],
            v2_send.at[r, dk],
            v2_recv.at[hi],
            device(k * ratio + r, lo, k_at(dk)),
        )

    for r in range(ratio):
        for dk in range(n_head):
            if dk:
                x2_copy(r, dk).start()
            else:

                @pl.when(k * ratio + r != hi)
                def _():
                    x2_copy(r, 0).start()

    x1[lo, k] = vals1[lo]
    for dl in range(n_lo):
        for dk in range(n_head):
            if dl or dk:
                start(
                    remote(
                        vals1.at[lo_at(dl)],
                        x1.at[lo, k],
                        v1_send.at[dl, dk],
                        v1_recv.at[dl, dk],
                        device(hi, lo_at(dl), k_at(dk)),
                    )
                )

    w2_copy.wait()
    for d in range(1, n_lo):
        arrived(
            w2.at[pl.ds(pl.multiple_of(lo_at(-d) * VDIM, VDIM), VDIM), :], w2_recv.at[d]
        )
    for z in range(n_hi):

        @pl.when(jnp.logical_not(jnp.logical_and(mine, hi == z)))
        def _():
            arrived(x2.at[z], v2_recv.at[z])

    product = jnp.dot(
        x2[...].reshape(n_hi * tok, n_lo * VDIM), w2[...], preferred_element_type=jnp.float32
    )
    part2[...] = product.reshape(part2.shape)
    send2[...] = product.astype(jnp.bfloat16).reshape(send2.shape)
    for d in range(1, n_hi):
        start(
            remote(
                send2.at[hi_at(d)],
                got2.at[d],
                r2_send.at[d],
                r2_recv.at[d],
                device(hi_at(d), lo, k),
            )
        )

    w1_copy.wait()
    for d in range(1, n_hi):
        arrived(
            w1.at[pl.ds(pl.multiple_of(hi_at(-d) * VDIM, VDIM), VDIM), :], w1_recv.at[d]
        )
    for dl in range(n_lo):
        for dk in range(n_head):
            if dl or dk:
                arrived(x1.at[lo_at(-dl), k_at(-dk)], v1_recv.at[dl, dk])
    product = None
    depth = ratio * VDIM
    for kk in range(n_head):
        term = jnp.dot(
            x1[:, kk].reshape(n_lo * tok, depth),
            w1[pl.ds(kk * depth, depth), :],
            preferred_element_type=jnp.float32,
        )
        product = term if product is None else product + term
    part1[...] = product.reshape(part1.shape)
    send1[...] = product.astype(jnp.bfloat16).reshape(send1.shape)
    for d in range(1, n_lo):
        start(
            remote(
                send1.at[lo_at(d)],
                got1.at[d],
                r1_send.at[d],
                r1_recv.at[d],
                device(hi, lo_at(d), k),
            )
        )

    mixed = part1[lo]
    for d in range(1, n_lo):
        arrived(got1.at[d], r1_recv.at[d])
        mixed = mixed + got1[d].astype(jnp.float32)
    out_ref[:, pl.ds(0, cols1)] = mixed.astype(jnp.bfloat16)
    mixed = part2[hi]
    for d in range(1, n_hi):
        arrived(got2.at[d], r2_recv.at[d])
        mixed = mixed + got2[d].astype(jnp.float32)
    out_ref[:, pl.ds(cols1, out_ref.shape[1] - cols1)] = mixed.astype(jnp.bfloat16)

    for copy in sent:
        copy.wait_send()
    for r in range(ratio):
        for dk in range(n_head):
            if dk:
                x2_copy(r, dk).wait_send()
            else:

                @pl.when(k * ratio + r != hi)
                def _():
                    x2_copy(r, 0).wait_send()


def body(n_ctx, n_head, queries, latent, w_uv, w_out, pair_perm):
    n_hi, n_lo = split_ctx(n_ctx)
    tok, heads, width = queries.shape
    ratio = heads // n_lo
    columns = w_out.shape[1]
    cols1 = columns // 256 * 128
    cols2 = columns - cols1
    dims = (n_hi, n_lo, n_head, tok, heads, cols1)
    bf16, f32 = jnp.bfloat16, jnp.float32
    vmem, dma = pltpu.VMEM, pltpu.SemaphoreType.DMA
    anywhere = pl.BlockSpec(memory_space=pl.ANY)
    return pl.pallas_call(
        functools.partial(kernel, dims),
        out_shape=jax.ShapeDtypeStruct((tok, columns), bf16),
        in_specs=[
            pl.BlockSpec(memory_space=pltpu.SMEM),
            pl.BlockSpec(memory_space=vmem),
            anywhere,
            anywhere,
            anywhere,
        ],
        out_specs=pl.BlockSpec(memory_space=vmem),
        scratch_shapes=[
            vmem((tok * heads, width), bf16),
            vmem(w_uv.shape, bf16),
            vmem((n_ctx * tok, width), bf16),
            vmem((LAT // 128, tok * heads, 128), f32),
            vmem((n_hi * VDIM, cols1), bf16),
            vmem((n_lo * VDIM, cols2), bf16),
            vmem((n_lo, tok, ratio * VDIM), bf16),
            vmem((ratio, tok, n_lo * VDIM), bf16),
            vmem((n_lo, n_head, tok, ratio * VDIM), bf16),
            vmem((n_hi, tok, n_lo * VDIM), bf16),
            vmem((n_lo, tok, cols1), f32),
            vmem((n_hi, tok, cols2), f32),
            vmem((n_lo, tok, cols1), bf16),
            vmem((n_hi, tok, cols2), bf16),
            vmem((n_lo, tok, cols1), bf16),
            vmem((n_hi, tok, cols2), bf16),
            dma((4,)),
            dma((n_hi,)),
            dma((n_hi,)),
            dma((n_hi, n_lo)),
            dma((n_hi, n_lo)),
            dma((n_hi, n_lo)),
            dma((n_hi, n_lo)),
            dma((n_hi,)),
            dma((n_hi,)),
            dma((n_lo,)),
            dma((n_lo,)),
            dma((n_lo, n_head)),
            dma((n_lo, n_head)),
            dma((ratio, n_head)),
            dma((n_hi,)),
            dma((n_lo,)),
            dma((n_lo,)),
            dma((n_hi,)),
            dma((n_hi,)),
        ],
        compiler_params=pltpu.CompilerParams(
            collective_id=0, has_side_effects=True, vmem_limit_bytes=56 * 1024 * 1024
        ),
    )(pair_perm, latent, queries.reshape(tok * heads, width), w_uv, w_out)


def solution(mesh):
    placed = (P("ctx", "head", None), P("ctx", None), P("head", None, None), P("ctx", "head"), P())
    return jax.shard_map(
        functools.partial(body, mesh.shape["ctx"], mesh.shape["head"]),
        mesh=mesh,
        in_specs=placed,
        out_specs=P("ctx", "head"),
        check_vma=False,
    )
```

```python
import functools

import jax
import jax.numpy as jnp
from jax import lax
from jax.experimental import pallas as pl
from jax.experimental.pallas import tpu as pltpu
from jax.sharding import PartitionSpec as P

LAT = 512
VDIM = 128
MESH = pl.DeviceIdType.MESH

score_scale = 192.0 ** (-0.5)


def split_ctx(n_ctx):
    low = 1
    while low * low < n_ctx:
        low *= 2
    return n_ctx // low, low


def kernel(
    dims,
    perm_ref,
    lat_ref,
    q_hbm,
    uv_hbm,
    w_hbm,
    out_ref,
    q_ref,
    uv_ref,
    lat,
    ctx_f32,
    w1,
    w2,
    vals1,
    vals2,
    x1,
    x2,
    part1,
    part2,
    send1,
    send2,
    got1,
    got2,
    local_sems,
    hi_send,
    hi_recv,
    lo_send,
    lo_recv,
    core_send,
    core_recv,
    w1_send,
    w1_recv,
    w2_send,
    w2_recv,
    v1_send,
    v1_recv,
    v2_send,
    vf_send,
    v2_recv,
    r1_send,
    r1_recv,
    r2_send,
    r2_recv,
):
    n_hi, n_lo, n_head, tok, heads, cols1, chunks1, chunks2 = dims
    n_ctx = n_hi * n_lo
    ratio = heads // n_lo
    pieces = 2 if n_head == 2 else 1
    rows_piece = tok // pieces
    me = lax.axis_index("ctx")
    k = lax.axis_index("head")
    hi = me // n_lo
    lo = lax.rem(me, n_lo)

    def hi_at(d):
        return lax.rem(hi + (d + n_hi) % n_hi, n_hi)

    def lo_at(d):
        return lax.rem(lo + (d + n_lo) % n_lo, n_lo)

    def k_at(d):
        return lax.rem(k + (d + n_head) % n_head, n_head)

    def device(h, l, kk):
        return (h * n_lo + l, kk)

    def remote(src, dst, send, recv, target):
        return pltpu.make_async_remote_copy(
            src_ref=src,
            dst_ref=dst,
            send_sem=send,
            recv_sem=recv,
            device_id=target,
            device_id_type=MESH,
        )

    q_copy = pltpu.make_async_copy(q_hbm, q_ref, local_sems.at[0])
    uv_copy = pltpu.make_async_copy(uv_hbm, uv_ref, local_sems.at[1])
    w1_copy = pltpu.make_async_copy(
        w_hbm.at[:, pl.ds(0, cols1)],
        w1.at[pl.ds(pl.multiple_of(hi * VDIM, VDIM), VDIM), :],
        local_sems.at[2],
    )
    w2_copy = pltpu.make_async_copy(
        w_hbm.at[:, pl.ds(cols1, w_hbm.shape[1] - cols1)],
        w2.at[pl.ds(pl.multiple_of(lo * VDIM, VDIM), VDIM), :],
        local_sems.at[3],
    )

    partners = [(0, dl, dk) for dl in range(n_lo) for dk in range(n_head) if dl or dk]
    partners += [(dh, 0, dk) for dh in range(1, n_hi) for dk in range(n_head)]
    barrier = pltpu.get_barrier_semaphore()
    for dh, dl, dk in partners:
        pl.semaphore_signal(
            barrier,
            inc=1,
            device_id=device(hi_at(dh), lo_at(dl), k_at(dk)),
            device_id_type=MESH,
        )
    lat[pl.ds(pl.multiple_of(me * tok, tok), tok), :] = lat_ref[...]
    pl.semaphore_wait(barrier, len(partners))

    def piece(dh, dl, kk):
        owner = hi_at(-dh) * n_lo + lo_at(-dl)
        start = owner * tok
        if pieces > 1:
            start = start + kk * rows_piece
        return lat.at[pl.ds(pl.multiple_of(start, rows_piece), rows_piece), :]

    own = piece(0, 0, k)
    sent = []

    def start(copy):
        copy.start()
        sent.append(copy)

    def to_hi(d):
        return remote(own, own, hi_send.at[d], hi_recv.at[d], device(hi_at(d), lo, k))

    def to_lo(dh, d):
        block = piece(dh, 0, k)
        return remote(
            block, block, lo_send.at[dh, d], lo_recv.at[dh, d], device(hi, lo_at(d), k)
        )

    def to_core(dh, dl):
        block = piece(dh, dl, k)
        return remote(
            block, block, core_send.at[dh, dl], core_recv.at[dh, dl], device(hi, lo, k_at(1))
        )

    def arrived(block, recv):
        remote(block, block, recv, recv, device(hi, lo, k_at(1))).wait_recv()

    for d in range(1, n_hi):
        start(to_hi(d))
    for d in range(1, n_lo):
        start(to_lo(0, d))
    def w1_rows(source):
        return w1.at[pl.ds(pl.multiple_of(source * VDIM, VDIM), VDIM), :]

    def w2_rows(source):
        return w2.at[pl.ds(pl.multiple_of(source * VDIM, VDIM), VDIM), :]

    for copy in (q_copy, uv_copy, w1_copy, w2_copy):
        copy.start()
    for d in range(1, n_hi):
        arrived(piece(d, 0, k), hi_recv.at[d])
        for e in range(1, n_lo):
            start(to_lo(d, e))
        if pieces > 1:
            start(to_core(d, 0))
    for d in range(1, n_lo):
        start(
            remote(
                w_hbm.at[:, pl.ds(cols1, w_hbm.shape[1] - cols1)],
                w2_rows(lo),
                w2_send.at[d],
                w2_recv.at[d],
                device(hi, lo_at(d), k),
            )
        )
    for d in range(1, n_hi):
        start(
            remote(
                w_hbm.at[:, pl.ds(0, cols1)],
                w1_rows(hi),
                w1_send.at[d],
                w1_recv.at[d],
                device(hi_at(d), lo, k),
            )
        )
    for dh in range(n_hi):
        for dl in range(1, n_lo):
            arrived(piece(dh, dl, k), lo_recv.at[dh, dl])
            if pieces > 1:
                start(to_core(dh, dl))

    total = n_ctx * tok
    half = tok // 2
    key_ids = lax.broadcasted_iota(jnp.int32, (1, total), 1)
    holder = key_ids // tok
    pair = jnp.zeros((1, total), jnp.int32)
    for c in range(n_ctx):
        pair = jnp.where(holder == c, perm_ref[c], pair)
    within = lax.rem(key_ids, tok)
    key_pos = jnp.where(within >= half, 2 * n_ctx - 1 - pair, pair) * half + lax.rem(within, half)
    my_pair = perm_ref[me]

    q_copy.wait()
    uv_copy.wait()
    if pieces > 1:
        for dh in range(n_hi):
            for dl in range(n_lo):
                if dh or dl:
                    arrived(piece(dh, dl, k_at(1)), core_recv.at[dh, dl])

    all_rows = tok * heads
    rows = 256 if total <= 1024 else 64
    for first in range(0, all_rows, rows):
        row_tok = (first + lax.broadcasted_iota(jnp.int32, (rows, 1), 0)) // heads
        query_pos = jnp.where(
            row_tok >= half, 2 * n_ctx - 1 - my_pair, my_pair
        ) * half + lax.rem(row_tok, half)
        scores = (
            lax.dot_general(
                q_ref[pl.ds(first, rows), :],
                lat[...],
                (((1,), (1,)), ((), ())),
                preferred_element_type=jnp.float32,
            )
            * score_scale
        )
        scores = jnp.where(key_pos <= query_pos, scores, -1e30)
        weights = jnp.exp(scores - jnp.max(scores, axis=1, keepdims=True))
        mass = jnp.sum(weights, axis=1, keepdims=True)
        numerator = jnp.dot(
            weights.astype(jnp.bfloat16), lat[:, pl.ds(0, LAT)], preferred_element_type=jnp.float32
        )
        context = numerator / mass
        for j in range(LAT // 128):
            ctx_f32[j, pl.ds(first, rows), :] = context[:, j * 128 : (j + 1) * 128]

    for h in range(heads):
        context = jnp.concatenate(
            [ctx_f32[j, pl.ds(h, tok, stride=heads), :] for j in range(LAT // 128)], axis=1
        ).astype(jnp.bfloat16)
        value = jnp.dot(context, uv_ref[h], preferred_element_type=jnp.float32).astype(jnp.bfloat16)
        r, l = h // n_lo, h % n_lo
        vals1[l, :, pl.ds(r * VDIM, VDIM)] = value
        vals2[r, :, pl.ds(l * VDIM, VDIM)] = value

    owner_k = hi // ratio
    mine = k == owner_k

    @pl.when(mine)
    def _():
        x2[hi] = vals2[lax.rem(hi, ratio)]

    def x2_copy(r):
        return remote(
            vals2.at[r], x2.at[hi], v2_send.at[r], v2_recv.at[hi], device(k * ratio + r, lo, k)
        )

    def x2_hand_on(z, dk):
        return remote(
            x2.at[z], x2.at[z], vf_send.at[z, dk], v2_recv.at[z], device(hi, lo, k_at(dk))
        )

    for r in range(ratio):

        @pl.when(k * ratio + r != hi)
        def _():
            x2_copy(r).start()

    @pl.when(mine)
    def _():
        for dk in range(1, n_head):
            x2_hand_on(hi, dk).start()

    x1[lo, k] = vals1[lo]
    for dl in range(n_lo):
        for dk in range(n_head):
            if dl or dk:
                start(
                    remote(
                        vals1.at[lo_at(dl)],
                        x1.at[lo, k],
                        v1_send.at[dl, dk],
                        v1_recv.at[dl, dk],
                        device(hi, lo_at(dl), k_at(dk)),
                    )
                )

    w2_copy.wait()
    for d in range(1, n_lo):
        arrived(
            w2.at[pl.ds(pl.multiple_of(lo_at(-d) * VDIM, VDIM), VDIM), :], w2_recv.at[d]
        )
    @pl.when(mine)
    def _():
        for d in range(1, n_hi):
            z = hi_at(d)
            arrived(x2.at[z], v2_recv.at[z])
            for dk in range(1, n_head):
                x2_hand_on(z, dk).start()

    @pl.when(jnp.logical_not(mine))
    def _():
        for z in range(n_hi):
            arrived(x2.at[z], v2_recv.at[z])

    rows2 = x2[...].reshape(n_hi * tok, n_lo * VDIM)
    for c, (first, size) in enumerate(chunks2):
        cols = pl.ds(first, size)
        product = jnp.dot(rows2, w2[:, cols], preferred_element_type=jnp.float32)
        product = product.reshape(n_hi, tok, size)
        part2[:, :, cols] = product
        send2[:, :, cols] = product.astype(jnp.bfloat16)
        for d in range(1, n_hi):
            start(
                remote(
                    send2.at[hi_at(d), :, cols],
                    got2.at[d, :, cols],
                    r2_send.at[c, d],
                    r2_recv.at[c, d],
                    device(hi_at(d), lo, k),
                )
            )

    w1_copy.wait()
    for d in range(1, n_hi):
        arrived(w1_rows(hi_at(-d)), w1_recv.at[d])
    for dl in range(n_lo):
        for dk in range(n_head):
            if dl or dk:
                arrived(x1.at[lo_at(-dl), k_at(-dk)], v1_recv.at[dl, dk])
    depth = ratio * VDIM
    rows1 = [x1[:, kk].reshape(n_lo * tok, depth) for kk in range(n_head)]
    for c, (first, size) in enumerate(chunks1):
        cols = pl.ds(first, size)
        product = None
        for kk in range(n_head):
            term = jnp.dot(
                rows1[kk], w1[pl.ds(kk * depth, depth), cols], preferred_element_type=jnp.float32
            )
            product = term if product is None else product + term
        product = product.reshape(n_lo, tok, size)
        part1[:, :, cols] = product
        send1[:, :, cols] = product.astype(jnp.bfloat16)
        for d in range(1, n_lo):
            start(
                remote(
                    send1.at[lo_at(d), :, cols],
                    got1.at[d, :, cols],
                    r1_send.at[c, d],
                    r1_recv.at[c, d],
                    device(hi, lo_at(d), k),
                )
            )

    def add_up(part, mine_at, got, recv, chunks, n, base):
        for c, (first, size) in enumerate(chunks):
            cols = pl.ds(first, size)
            mixed = part[mine_at, :, cols]
            for d in range(1, n):
                arrived(got.at[d, :, cols], recv.at[c, d])
                mixed = mixed + got[d, :, cols].astype(jnp.float32)
            out_ref[:, pl.ds(base + first, size)] = mixed.astype(jnp.bfloat16)

    add_up(part1, lo, got1, r1_recv, chunks1, n_lo, 0)
    add_up(part2, hi, got2, r2_recv, chunks2, n_hi, cols1)

    for copy in sent:
        copy.wait_send()
    for r in range(ratio):

        @pl.when(k * ratio + r != hi)
        def _():
            x2_copy(r).wait_send()

    @pl.when(mine)
    def _():
        for z in range(n_hi):
            for dk in range(1, n_head):
                x2_hand_on(z, dk).wait_send()


def body(n_ctx, n_head, queries, latent, w_uv, w_out, pair_perm):
    n_hi, n_lo = split_ctx(n_ctx)
    tok, heads, width = queries.shape
    ratio = heads // n_lo
    columns = w_out.shape[1]
    cols1 = columns // 128 * 6 // 14 * 128
    cols2 = columns - cols1
    chunks1, chunks2 = [(0, cols1)], [(0, cols2)]
    dims = (n_hi, n_lo, n_head, tok, heads, cols1, chunks1, chunks2)
    bf16, f32 = jnp.bfloat16, jnp.float32
    vmem, dma = pltpu.VMEM, pltpu.SemaphoreType.DMA
    anywhere = pl.BlockSpec(memory_space=pl.ANY)
    return pl.pallas_call(
        functools.partial(kernel, dims),
        out_shape=jax.ShapeDtypeStruct((tok, columns), bf16),
        in_specs=[
            pl.BlockSpec(memory_space=pltpu.SMEM),
            pl.BlockSpec(memory_space=vmem),
            anywhere,
            anywhere,
            anywhere,
        ],
        out_specs=pl.BlockSpec(memory_space=vmem),
        scratch_shapes=[
            vmem((tok * heads, width), bf16),
            vmem(w_uv.shape, bf16),
            vmem((n_ctx * tok, width), bf16),
            vmem((LAT // 128, tok * heads, 128), f32),
            vmem((n_hi * VDIM, cols1), bf16),
            vmem((n_lo * VDIM, cols2), bf16),
            vmem((n_lo, tok, ratio * VDIM), bf16),
            vmem((ratio, tok, n_lo * VDIM), bf16),
            vmem((n_lo, n_head, tok, ratio * VDIM), bf16),
            vmem((n_hi, tok, n_lo * VDIM), bf16),
            vmem((n_lo, tok, cols1), f32),
            vmem((n_hi, tok, cols2), f32),
            vmem((n_lo, tok, cols1), bf16),
            vmem((n_hi, tok, cols2), bf16),
            vmem((n_lo, tok, cols1), bf16),
            vmem((n_hi, tok, cols2), bf16),
            dma((4,)),
            dma((n_hi,)),
            dma((n_hi,)),
            dma((n_hi, n_lo)),
            dma((n_hi, n_lo)),
            dma((n_hi, n_lo)),
            dma((n_hi, n_lo)),
            dma((n_hi,)),
            dma((n_hi,)),
            dma((n_lo,)),
            dma((n_lo,)),
            dma((n_lo, n_head)),
            dma((n_lo, n_head)),
            dma((ratio,)),
            dma((n_hi, n_head)),
            dma((n_hi,)),
            dma((len(chunks1), n_lo)),
            dma((len(chunks1), n_lo)),
            dma((len(chunks2), n_hi)),
            dma((len(chunks2), n_hi)),
        ],
        compiler_params=pltpu.CompilerParams(
            collective_id=0, has_side_effects=True, vmem_limit_bytes=56 * 1024 * 1024
        ),
    )(pair_perm, latent, queries.reshape(tok * heads, width), w_uv, w_out)


def solution(mesh):
    placed = (P("ctx", "head", None), P("ctx", None), P("head", None, None), P("ctx", "head"), P())
    return jax.shard_map(
        functools.partial(body, mesh.shape["ctx"], mesh.shape["head"]),
        mesh=mesh,
        in_specs=placed,
        out_specs=P("ctx", "head"),
        check_vma=False,
    )
```

```python
import functools

import jax
import jax.numpy as jnp
from jax import lax
from jax.experimental import pallas as pl
from jax.experimental.pallas import tpu as pltpu
from jax.sharding import PartitionSpec as P

LAT = 512
VDIM = 128
MESH = pl.DeviceIdType.MESH

score_scale = 192.0 ** (-0.5)


def split_ctx(n_ctx):
    low = 1
    while low * low < n_ctx:
        low *= 2
    return n_ctx // low, low


def kernel(
    dims,
    perm_ref,
    lat_ref,
    q_hbm,
    uv_hbm,
    w_hbm,
    out_ref,
    q_ref,
    uv_ref,
    lat,
    ctx_f32,
    w1,
    w2,
    vals1,
    vals2,
    x1,
    x2,
    part1,
    part2,
    send1,
    send2,
    got1,
    got2,
    local_sems,
    hi_send,
    hi_recv,
    lo_send,
    lo_recv,
    core_send,
    core_recv,
    w1_send,
    w1_recv,
    w2_send,
    w2_recv,
    v1_send,
    v1_recv,
    v2_send,
    vf_send,
    v2_recv,
    r1_send,
    r1_recv,
    r2_send,
    r2_recv,
):
    n_hi, n_lo, n_head, tok, heads, cols1, chunks1, chunks2 = dims
    n_ctx = n_hi * n_lo
    ratio = heads // n_lo
    pieces = 2 if n_head == 2 else 1
    rows_piece = tok // pieces
    me = lax.axis_index("ctx")
    k = lax.axis_index("head")
    hi = me // n_lo
    lo = lax.rem(me, n_lo)

    def hi_at(d):
        return lax.rem(hi + (d + n_hi) % n_hi, n_hi)

    def lo_at(d):
        return lax.rem(lo + (d + n_lo) % n_lo, n_lo)

    def k_at(d):
        return lax.rem(k + (d + n_head) % n_head, n_head)

    def device(h, l, kk):
        return (h * n_lo + l, kk)

    def remote(src, dst, send, recv, target):
        return pltpu.make_async_remote_copy(
            src_ref=src,
            dst_ref=dst,
            send_sem=send,
            recv_sem=recv,
            device_id=target,
            device_id_type=MESH,
        )

    q_copy = pltpu.make_async_copy(q_hbm, q_ref, local_sems.at[0])
    uv_copy = pltpu.make_async_copy(uv_hbm, uv_ref, local_sems.at[1])
    w1_copy = pltpu.make_async_copy(
        w_hbm.at[:, pl.ds(0, cols1)],
        w1.at[pl.ds(pl.multiple_of(hi * VDIM, VDIM), VDIM), :],
        local_sems.at[2],
    )
    w2_copy = pltpu.make_async_copy(
        w_hbm.at[:, pl.ds(cols1, w_hbm.shape[1] - cols1)],
        w2.at[pl.ds(pl.multiple_of(lo * VDIM, VDIM), VDIM), :],
        local_sems.at[3],
    )

    partners = [(0, dl, dk) for dl in range(n_lo) for dk in range(n_head) if dl or dk]
    partners += [(dh, 0, dk) for dh in range(1, n_hi) for dk in range(n_head)]
    barrier = pltpu.get_barrier_semaphore()
    for dh, dl, dk in partners:
        pl.semaphore_signal(
            barrier,
            inc=1,
            device_id=device(hi_at(dh), lo_at(dl), k_at(dk)),
            device_id_type=MESH,
        )
    lat[pl.ds(pl.multiple_of(me * tok, tok), tok), :] = lat_ref[...]
    pl.semaphore_wait(barrier, len(partners))

    def piece(dh, dl, kk):
        owner = hi_at(-dh) * n_lo + lo_at(-dl)
        start = owner * tok
        if pieces > 1:
            start = start + kk * rows_piece
        return lat.at[pl.ds(pl.multiple_of(start, rows_piece), rows_piece), :]

    own = piece(0, 0, k)
    sent = []

    def start(copy):
        copy.start()
        sent.append(copy)

    def to_hi(d):
        return remote(own, own, hi_send.at[d], hi_recv.at[d], device(hi_at(d), lo, k))

    def to_lo(dh, d):
        block = piece(dh, 0, k)
        return remote(
            block, block, lo_send.at[dh, d], lo_recv.at[dh, d], device(hi, lo_at(d), k)
        )

    def to_core(dh, dl):
        block = piece(dh, dl, k)
        return remote(
            block, block, core_send.at[dh, dl], core_recv.at[dh, dl], device(hi, lo, k_at(1))
        )

    def arrived(block, recv):
        remote(block, block, recv, recv, device(hi, lo, k_at(1))).wait_recv()

    for d in range(1, n_hi):
        start(to_hi(d))
    for d in range(1, n_lo):
        start(to_lo(0, d))
    part_rows = VDIM // 2

    def w1_rows(source, h):
        start = source * VDIM + h * part_rows
        return w1.at[pl.ds(pl.multiple_of(start, part_rows), part_rows), :]

    def w2_rows(source, h):
        start = source * VDIM + h * part_rows
        return w2.at[pl.ds(pl.multiple_of(start, part_rows), part_rows), :]

    def send_w1(h):
        for d in range(1, n_hi):
            start(
                remote(
                    w_hbm.at[pl.ds(h * part_rows, part_rows), pl.ds(0, cols1)],
                    w1_rows(hi, h),
                    w1_send.at[h, d],
                    w1_recv.at[h, d],
                    device(hi_at(d), lo, k),
                )
            )

    def send_w2(h):
        for d in range(1, n_lo):
            start(
                remote(
                    w_hbm.at[
                        pl.ds(h * part_rows, part_rows),
                        pl.ds(cols1, w_hbm.shape[1] - cols1),
                    ],
                    w2_rows(lo, h),
                    w2_send.at[h, d],
                    w2_recv.at[h, d],
                    device(hi, lo_at(d), k),
                )
            )

    send_w1(0)
    for copy in (q_copy, uv_copy, w1_copy, w2_copy):
        copy.start()
    for d in range(1, n_hi):
        arrived(piece(d, 0, k), hi_recv.at[d])
        for e in range(1, n_lo):
            start(to_lo(d, e))
        if pieces > 1:
            start(to_core(d, 0))
    send_w2(0)
    send_w2(1)
    send_w1(1)
    for dh in range(n_hi):
        for dl in range(1, n_lo):
            arrived(piece(dh, dl, k), lo_recv.at[dh, dl])
            if pieces > 1:
                start(to_core(dh, dl))

    total = n_ctx * tok
    half = tok // 2
    key_ids = lax.broadcasted_iota(jnp.int32, (1, total), 1)
    holder = key_ids // tok
    pair = jnp.zeros((1, total), jnp.int32)
    for c in range(n_ctx):
        pair = jnp.where(holder == c, perm_ref[c], pair)
    within = lax.rem(key_ids, tok)
    key_pos = jnp.where(within >= half, 2 * n_ctx - 1 - pair, pair) * half + lax.rem(within, half)
    my_pair = perm_ref[me]

    q_copy.wait()
    uv_copy.wait()
    if pieces > 1:
        for dh in range(n_hi):
            for dl in range(n_lo):
                if dh or dl:
                    arrived(piece(dh, dl, k_at(1)), core_recv.at[dh, dl])

    all_rows = tok * heads
    rows = 256 if total <= 1024 else 64
    for first in range(0, all_rows, rows):
        row_tok = (first + lax.broadcasted_iota(jnp.int32, (rows, 1), 0)) // heads
        query_pos = jnp.where(
            row_tok >= half, 2 * n_ctx - 1 - my_pair, my_pair
        ) * half + lax.rem(row_tok, half)
        scores = (
            lax.dot_general(
                q_ref[pl.ds(first, rows), :],
                lat[...],
                (((1,), (1,)), ((), ())),
                preferred_element_type=jnp.float32,
            )
            * score_scale
        )
        scores = jnp.where(key_pos <= query_pos, scores, -1e30)
        weights = jnp.exp(scores - jnp.max(scores, axis=1, keepdims=True))
        mass = jnp.sum(weights, axis=1, keepdims=True)
        numerator = jnp.dot(
            weights.astype(jnp.bfloat16), lat[:, pl.ds(0, LAT)], preferred_element_type=jnp.float32
        )
        context = numerator / mass
        for j in range(LAT // 128):
            ctx_f32[j, pl.ds(first, rows), :] = context[:, j * 128 : (j + 1) * 128]

    for h in range(heads):
        context = jnp.concatenate(
            [ctx_f32[j, pl.ds(h, tok, stride=heads), :] for j in range(LAT // 128)], axis=1
        ).astype(jnp.bfloat16)
        value = jnp.dot(context, uv_ref[h], preferred_element_type=jnp.float32).astype(jnp.bfloat16)
        r, l = h // n_lo, h % n_lo
        vals1[l, :, pl.ds(r * VDIM, VDIM)] = value
        vals2[r, :, pl.ds(l * VDIM, VDIM)] = value

    owner_k = hi // ratio
    mine = k == owner_k

    @pl.when(mine)
    def _():
        x2[hi] = vals2[lax.rem(hi, ratio)]

    def x2_copy(r):
        return remote(
            vals2.at[r], x2.at[hi], v2_send.at[r], v2_recv.at[hi], device(k * ratio + r, lo, k)
        )

    def x2_hand_on(z, dk):
        return remote(
            x2.at[z], x2.at[z], vf_send.at[z, dk], v2_recv.at[z], device(hi, lo, k_at(dk))
        )

    for r in range(ratio):

        @pl.when(k * ratio + r != hi)
        def _():
            x2_copy(r).start()

    @pl.when(mine)
    def _():
        for dk in range(1, n_head):
            x2_hand_on(hi, dk).start()

    x1[lo, k] = vals1[lo]
    for dl in range(n_lo):
        for dk in range(n_head):
            if dl or dk:
                start(
                    remote(
                        vals1.at[lo_at(dl)],
                        x1.at[lo, k],
                        v1_send.at[dl, dk],
                        v1_recv.at[dl, dk],
                        device(hi, lo_at(dl), k_at(dk)),
                    )
                )

    w2_copy.wait()
    for h in range(2):
        for d in range(1, n_lo):
            arrived(w2_rows(lo_at(-d), h), w2_recv.at[h, d])
    @pl.when(mine)
    def _():
        for d in range(1, n_hi):
            z = hi_at(d)
            arrived(x2.at[z], v2_recv.at[z])
            for dk in range(1, n_head):
                x2_hand_on(z, dk).start()

    @pl.when(jnp.logical_not(mine))
    def _():
        for z in range(n_hi):
            arrived(x2.at[z], v2_recv.at[z])

    rows2 = x2[...].reshape(n_hi * tok, n_lo * VDIM)
    for c, (first, size) in enumerate(chunks2):
        cols = pl.ds(first, size)
        product = jnp.dot(rows2, w2[:, cols], preferred_element_type=jnp.float32)
        product = product.reshape(n_hi, tok, size)
        part2[:, :, cols] = product
        send2[:, :, cols] = product.astype(jnp.bfloat16)
        for d in range(1, n_hi):
            start(
                remote(
                    send2.at[hi_at(d), :, cols],
                    got2.at[d, :, cols],
                    r2_send.at[c, d],
                    r2_recv.at[c, d],
                    device(hi_at(d), lo, k),
                )
            )

    w1_copy.wait()
    for h in range(2):
        for d in range(1, n_hi):
            arrived(w1_rows(hi_at(-d), h), w1_recv.at[h, d])
    for dl in range(n_lo):
        for dk in range(n_head):
            if dl or dk:
                arrived(x1.at[lo_at(-dl), k_at(-dk)], v1_recv.at[dl, dk])
    depth = ratio * VDIM
    rows1 = [x1[:, kk].reshape(n_lo * tok, depth) for kk in range(n_head)]
    for c, (first, size) in enumerate(chunks1):
        cols = pl.ds(first, size)
        product = None
        for kk in range(n_head):
            term = jnp.dot(
                rows1[kk], w1[pl.ds(kk * depth, depth), cols], preferred_element_type=jnp.float32
            )
            product = term if product is None else product + term
        product = product.reshape(n_lo, tok, size)
        part1[:, :, cols] = product
        send1[:, :, cols] = product.astype(jnp.bfloat16)
        for d in range(1, n_lo):
            start(
                remote(
                    send1.at[lo_at(d), :, cols],
                    got1.at[d, :, cols],
                    r1_send.at[c, d],
                    r1_recv.at[c, d],
                    device(hi, lo_at(d), k),
                )
            )

    def add_up(part, mine_at, got, recv, chunks, n, base):
        for c, (first, size) in enumerate(chunks):
            cols = pl.ds(first, size)
            mixed = part[mine_at, :, cols]
            for d in range(1, n):
                arrived(got.at[d, :, cols], recv.at[c, d])
                mixed = mixed + got[d, :, cols].astype(jnp.float32)
            out_ref[:, pl.ds(base + first, size)] = mixed.astype(jnp.bfloat16)

    add_up(part1, lo, got1, r1_recv, chunks1, n_lo, 0)
    add_up(part2, hi, got2, r2_recv, chunks2, n_hi, cols1)

    for copy in sent:
        copy.wait_send()
    for r in range(ratio):

        @pl.when(k * ratio + r != hi)
        def _():
            x2_copy(r).wait_send()

    @pl.when(mine)
    def _():
        for z in range(n_hi):
            for dk in range(1, n_head):
                x2_hand_on(z, dk).wait_send()


def body(n_ctx, n_head, queries, latent, w_uv, w_out, pair_perm):
    n_hi, n_lo = split_ctx(n_ctx)
    tok, heads, width = queries.shape
    ratio = heads // n_lo
    columns = w_out.shape[1]
    cols1 = columns // 128 * 6 // 14 * 128
    cols2 = columns - cols1
    chunks1, chunks2 = [(0, cols1)], [(0, cols2)]
    dims = (n_hi, n_lo, n_head, tok, heads, cols1, chunks1, chunks2)
    bf16, f32 = jnp.bfloat16, jnp.float32
    vmem, dma = pltpu.VMEM, pltpu.SemaphoreType.DMA
    anywhere = pl.BlockSpec(memory_space=pl.ANY)
    return pl.pallas_call(
        functools.partial(kernel, dims),
        out_shape=jax.ShapeDtypeStruct((tok, columns), bf16),
        in_specs=[
            pl.BlockSpec(memory_space=pltpu.SMEM),
            pl.BlockSpec(memory_space=vmem),
            anywhere,
            anywhere,
            anywhere,
        ],
        out_specs=pl.BlockSpec(memory_space=vmem),
        scratch_shapes=[
            vmem((tok * heads, width), bf16),
            vmem(w_uv.shape, bf16),
            vmem((n_ctx * tok, width), bf16),
            vmem((LAT // 128, tok * heads, 128), f32),
            vmem((n_hi * VDIM, cols1), bf16),
            vmem((n_lo * VDIM, cols2), bf16),
            vmem((n_lo, tok, ratio * VDIM), bf16),
            vmem((ratio, tok, n_lo * VDIM), bf16),
            vmem((n_lo, n_head, tok, ratio * VDIM), bf16),
            vmem((n_hi, tok, n_lo * VDIM), bf16),
            vmem((n_lo, tok, cols1), f32),
            vmem((n_hi, tok, cols2), f32),
            vmem((n_lo, tok, cols1), bf16),
            vmem((n_hi, tok, cols2), bf16),
            vmem((n_lo, tok, cols1), bf16),
            vmem((n_hi, tok, cols2), bf16),
            dma((4,)),
            dma((n_hi,)),
            dma((n_hi,)),
            dma((n_hi, n_lo)),
            dma((n_hi, n_lo)),
            dma((n_hi, n_lo)),
            dma((n_hi, n_lo)),
            dma((2, n_hi)),
            dma((2, n_hi)),
            dma((2, n_lo)),
            dma((2, n_lo)),
            dma((n_lo, n_head)),
            dma((n_lo, n_head)),
            dma((ratio,)),
            dma((n_hi, n_head)),
            dma((n_hi,)),
            dma((len(chunks1), n_lo)),
            dma((len(chunks1), n_lo)),
            dma((len(chunks2), n_hi)),
            dma((len(chunks2), n_hi)),
        ],
        compiler_params=pltpu.CompilerParams(
            collective_id=0, has_side_effects=True, vmem_limit_bytes=56 * 1024 * 1024
        ),
    )(pair_perm, latent, queries.reshape(tok * heads, width), w_uv, w_out)


def solution(mesh):
    placed = (P("ctx", "head", None), P("ctx", None), P("head", None, None), P("ctx", "head"), P())
    return jax.shard_map(
        functools.partial(body, mesh.shape["ctx"], mesh.shape["head"]),
        mesh=mesh,
        in_specs=placed,
        out_specs=P("ctx", "head"),
        check_vma=False,
    )
```

```python
import functools

import jax
import jax.numpy as jnp
from jax import lax
from jax.experimental import pallas as pl
from jax.experimental.pallas import tpu as pltpu
from jax.sharding import PartitionSpec as P

LAT = 512
VDIM = 128
MESH = pl.DeviceIdType.MESH

score_scale = 192.0 ** (-0.5)


def split_ctx(n_ctx):
    low = 1
    while low * low < n_ctx:
        low *= 2
    return n_ctx // low, low


def kernel(
    dims,
    perm_ref,
    lat_ref,
    q_hbm,
    uv_hbm,
    w_hbm,
    out_ref,
    q_ref,
    uv_ref,
    lat,
    ctx_f32,
    w1,
    w2,
    vals1,
    vals2,
    x1,
    x2,
    part1,
    part2,
    send1,
    send2,
    got1,
    got2,
    local_sems,
    hi_send,
    hi_recv,
    lo_send,
    lo_recv,
    core_send,
    core_recv,
    w1_send,
    w1_recv,
    w2_send,
    w2_recv,
    v1_send,
    v1_recv,
    v2_send,
    vf_send,
    v2_recv,
    r1_send,
    r1_recv,
    r2_send,
    r2_recv,
):
    n_hi, n_lo, n_head, tok, heads, cols1, chunks1, chunks2 = dims
    n_ctx = n_hi * n_lo
    ratio = heads // n_lo
    pieces = 2 if n_head == 2 else 1
    rows_piece = tok // pieces
    me = lax.axis_index("ctx")
    k = lax.axis_index("head")
    hi = me // n_lo
    lo = lax.rem(me, n_lo)

    def hi_at(d):
        return lax.rem(hi + (d + n_hi) % n_hi, n_hi)

    def lo_at(d):
        return lax.rem(lo + (d + n_lo) % n_lo, n_lo)

    def k_at(d):
        return lax.rem(k + (d + n_head) % n_head, n_head)

    def device(h, l, kk):
        return (h * n_lo + l, kk)

    def remote(src, dst, send, recv, target):
        return pltpu.make_async_remote_copy(
            src_ref=src,
            dst_ref=dst,
            send_sem=send,
            recv_sem=recv,
            device_id=target,
            device_id_type=MESH,
        )

    q_copy = pltpu.make_async_copy(q_hbm, q_ref, local_sems.at[0])
    uv_copy = pltpu.make_async_copy(uv_hbm, uv_ref, local_sems.at[1])
    w1_copy = pltpu.make_async_copy(
        w_hbm.at[:, pl.ds(0, cols1)],
        w1.at[pl.ds(pl.multiple_of(hi * VDIM, VDIM), VDIM), :],
        local_sems.at[2],
    )
    w2_copy = pltpu.make_async_copy(
        w_hbm.at[:, pl.ds(cols1, w_hbm.shape[1] - cols1)],
        w2.at[pl.ds(pl.multiple_of(lo * VDIM, VDIM), VDIM), :],
        local_sems.at[3],
    )

    partners = [(0, dl, dk) for dl in range(n_lo) for dk in range(n_head) if dl or dk]
    partners += [(dh, 0, dk) for dh in range(1, n_hi) for dk in range(n_head)]
    barrier = pltpu.get_barrier_semaphore()
    for dh, dl, dk in partners:
        pl.semaphore_signal(
            barrier,
            inc=1,
            device_id=device(hi_at(dh), lo_at(dl), k_at(dk)),
            device_id_type=MESH,
        )
    lat[pl.ds(pl.multiple_of(me * tok, tok), tok), :] = lat_ref[...]
    pl.semaphore_wait(barrier, len(partners))

    def piece(dh, dl, kk):
        owner = hi_at(-dh) * n_lo + lo_at(-dl)
        start = owner * tok
        if pieces > 1:
            start = start + kk * rows_piece
        return lat.at[pl.ds(pl.multiple_of(start, rows_piece), rows_piece), :]

    own = piece(0, 0, k)
    sent = []

    def start(copy):
        copy.start()
        sent.append(copy)

    def to_hi(d):
        return remote(own, own, hi_send.at[d], hi_recv.at[d], device(hi_at(d), lo, k))

    def to_lo(dh, d):
        block = piece(dh, 0, k)
        return remote(
            block, block, lo_send.at[dh, d], lo_recv.at[dh, d], device(hi, lo_at(d), k)
        )

    def to_core(dh, dl):
        block = piece(dh, dl, k)
        return remote(
            block, block, core_send.at[dh, dl], core_recv.at[dh, dl], device(hi, lo, k_at(1))
        )

    def arrived(block, recv):
        remote(block, block, recv, recv, device(hi, lo, k_at(1))).wait_recv()

    for d in range(1, n_hi):
        start(to_hi(d))
    for d in range(1, n_lo):
        start(to_lo(0, d))
    part_rows = VDIM // 2

    def w1_rows(source, h):
        start = source * VDIM + h * part_rows
        return w1.at[pl.ds(pl.multiple_of(start, part_rows), part_rows), :]

    def w2_rows(source, h):
        start = source * VDIM + h * part_rows
        return w2.at[pl.ds(pl.multiple_of(start, part_rows), part_rows), :]

    def send_w1(h):
        for d in range(1, n_hi):
            start(
                remote(
                    w_hbm.at[pl.ds(h * part_rows, part_rows), pl.ds(0, cols1)],
                    w1_rows(hi, h),
                    w1_send.at[h, d],
                    w1_recv.at[h, d],
                    device(hi_at(d), lo, k),
                )
            )

    def send_w2(h):
        for d in range(1, n_lo):
            start(
                remote(
                    w_hbm.at[
                        pl.ds(h * part_rows, part_rows),
                        pl.ds(cols1, w_hbm.shape[1] - cols1),
                    ],
                    w2_rows(lo, h),
                    w2_send.at[h, d],
                    w2_recv.at[h, d],
                    device(hi, lo_at(d), k),
                )
            )

    send_w1(0)
    for copy in (q_copy, uv_copy, w1_copy, w2_copy):
        copy.start()
    for d in range(1, n_hi):
        arrived(piece(d, 0, k), hi_recv.at[d])
        for e in range(1, n_lo):
            start(to_lo(d, e))
        if pieces > 1:
            start(to_core(d, 0))
    send_w2(0)
    send_w2(1)
    send_w1(1)
    for dh in range(n_hi):
        for dl in range(1, n_lo):
            arrived(piece(dh, dl, k), lo_recv.at[dh, dl])
            if pieces > 1:
                start(to_core(dh, dl))

    total = n_ctx * tok
    half = tok // 2
    key_ids = lax.broadcasted_iota(jnp.int32, (1, total), 1)
    holder = key_ids // tok
    pair = jnp.zeros((1, total), jnp.int32)
    for c in range(n_ctx):
        pair = jnp.where(holder == c, perm_ref[c], pair)
    within = lax.rem(key_ids, tok)
    key_pos = jnp.where(within >= half, 2 * n_ctx - 1 - pair, pair) * half + lax.rem(within, half)
    my_pair = perm_ref[me]

    q_copy.wait()
    uv_copy.wait()
    if pieces > 1:
        for dh in range(n_hi):
            for dl in range(n_lo):
                if dh or dl:
                    arrived(piece(dh, dl, k_at(1)), core_recv.at[dh, dl])

    all_rows = tok * heads
    rows = 256 if total <= 1024 else 64
    for first in range(0, all_rows, rows):
        row_tok = (first + lax.broadcasted_iota(jnp.int32, (rows, 1), 0)) // heads
        query_pos = jnp.where(
            row_tok >= half, 2 * n_ctx - 1 - my_pair, my_pair
        ) * half + lax.rem(row_tok, half)
        scores = (
            lax.dot_general(
                q_ref[pl.ds(first, rows), :],
                lat[...],
                (((1,), (1,)), ((), ())),
                preferred_element_type=jnp.float32,
            )
            * score_scale
        )
        scores = jnp.where(key_pos <= query_pos, scores, -1e30)
        weights = jnp.exp(scores - jnp.max(scores, axis=1, keepdims=True))
        mass = jnp.sum(weights, axis=1, keepdims=True)
        numerator = jnp.dot(
            weights.astype(jnp.bfloat16), lat[:, pl.ds(0, LAT)], preferred_element_type=jnp.float32
        )
        context = numerator / mass
        for j in range(LAT // 128):
            ctx_f32[j, pl.ds(first, rows), :] = context[:, j * 128 : (j + 1) * 128]

    def x2_copy(r):
        return remote(
            vals2.at[r], x2.at[hi], v2_send.at[r], v2_recv.at[hi], device(k * ratio + r, lo, k)
        )

    for h in range(heads):
        context = jnp.concatenate(
            [ctx_f32[j, pl.ds(h, tok, stride=heads), :] for j in range(LAT // 128)], axis=1
        ).astype(jnp.bfloat16)
        value = jnp.dot(context, uv_ref[h], preferred_element_type=jnp.float32).astype(jnp.bfloat16)
        r, l = h // n_lo, h % n_lo
        vals1[l, :, pl.ds(r * VDIM, VDIM)] = value
        vals2[r, :, pl.ds(l * VDIM, VDIM)] = value
        if l == n_lo - 1:

            @pl.when(k * ratio + r != hi)
            def _():
                x2_copy(r).start()


    owner_k = hi // ratio
    mine = k == owner_k

    @pl.when(mine)
    def _():
        x2[hi] = vals2[lax.rem(hi, ratio)]

    def x2_hand_on(z, dk):
        return remote(
            x2.at[z], x2.at[z], vf_send.at[z, dk], v2_recv.at[z], device(hi, lo, k_at(dk))
        )

    @pl.when(mine)
    def _():
        for dk in range(1, n_head):
            x2_hand_on(hi, dk).start()

    x1[lo, k] = vals1[lo]
    for dl in range(n_lo):
        for dk in range(n_head):
            if dl or dk:
                start(
                    remote(
                        vals1.at[lo_at(dl)],
                        x1.at[lo, k],
                        v1_send.at[dl, dk],
                        v1_recv.at[dl, dk],
                        device(hi, lo_at(dl), k_at(dk)),
                    )
                )

    w2_copy.wait()
    for h in range(2):
        for d in range(1, n_lo):
            arrived(w2_rows(lo_at(-d), h), w2_recv.at[h, d])
    @pl.when(mine)
    def _():
        for d in range(1, n_hi):
            z = hi_at(d)
            arrived(x2.at[z], v2_recv.at[z])
            for dk in range(1, n_head):
                x2_hand_on(z, dk).start()

    @pl.when(jnp.logical_not(mine))
    def _():
        for z in range(n_hi):
            arrived(x2.at[z], v2_recv.at[z])

    rows2 = x2[...].reshape(n_hi * tok, n_lo * VDIM)
    for c, (first, size) in enumerate(chunks2):
        cols = pl.ds(first, size)
        product = jnp.dot(rows2, w2[:, cols], preferred_element_type=jnp.float32)
        product = product.reshape(n_hi, tok, size)
        part2[:, :, cols] = product
        send2[:, :, cols] = product.astype(jnp.bfloat16)
        for d in range(1, n_hi):
            start(
                remote(
                    send2.at[hi_at(d), :, cols],
                    got2.at[d, :, cols],
                    r2_send.at[c, d],
                    r2_recv.at[c, d],
                    device(hi_at(d), lo, k),
                )
            )

    w1_copy.wait()
    for h in range(2):
        for d in range(1, n_hi):
            arrived(w1_rows(hi_at(-d), h), w1_recv.at[h, d])
    for dl in range(n_lo):
        for dk in range(n_head):
            if dl or dk:
                arrived(x1.at[lo_at(-dl), k_at(-dk)], v1_recv.at[dl, dk])
    depth = ratio * VDIM
    rows1 = [x1[:, kk].reshape(n_lo * tok, depth) for kk in range(n_head)]
    for c, (first, size) in enumerate(chunks1):
        cols = pl.ds(first, size)
        product = None
        for kk in range(n_head):
            term = jnp.dot(
                rows1[kk], w1[pl.ds(kk * depth, depth), cols], preferred_element_type=jnp.float32
            )
            product = term if product is None else product + term
        product = product.reshape(n_lo, tok, size)
        part1[:, :, cols] = product
        send1[:, :, cols] = product.astype(jnp.bfloat16)
        for d in range(1, n_lo):
            start(
                remote(
                    send1.at[lo_at(d), :, cols],
                    got1.at[d, :, cols],
                    r1_send.at[c, d],
                    r1_recv.at[c, d],
                    device(hi, lo_at(d), k),
                )
            )

    def add_up(part, mine_at, got, recv, chunks, n, base):
        for c, (first, size) in enumerate(chunks):
            cols = pl.ds(first, size)
            mixed = part[mine_at, :, cols]
            for d in range(1, n):
                arrived(got.at[d, :, cols], recv.at[c, d])
                mixed = mixed + got[d, :, cols].astype(jnp.float32)
            out_ref[:, pl.ds(base + first, size)] = mixed.astype(jnp.bfloat16)

    add_up(part1, lo, got1, r1_recv, chunks1, n_lo, 0)
    add_up(part2, hi, got2, r2_recv, chunks2, n_hi, cols1)

    for copy in sent:
        copy.wait_send()
    for r in range(ratio):

        @pl.when(k * ratio + r != hi)
        def _():
            x2_copy(r).wait_send()

    @pl.when(mine)
    def _():
        for z in range(n_hi):
            for dk in range(1, n_head):
                x2_hand_on(z, dk).wait_send()


def body(n_ctx, n_head, queries, latent, w_uv, w_out, pair_perm):
    n_hi, n_lo = split_ctx(n_ctx)
    tok, heads, width = queries.shape
    ratio = heads // n_lo
    columns = w_out.shape[1]
    cols1 = columns // 128 * 6 // 14 * 128
    cols2 = columns - cols1
    chunks1, chunks2 = [(0, cols1)], [(0, cols2)]
    dims = (n_hi, n_lo, n_head, tok, heads, cols1, chunks1, chunks2)
    bf16, f32 = jnp.bfloat16, jnp.float32
    vmem, dma = pltpu.VMEM, pltpu.SemaphoreType.DMA
    anywhere = pl.BlockSpec(memory_space=pl.ANY)
    return pl.pallas_call(
        functools.partial(kernel, dims),
        out_shape=jax.ShapeDtypeStruct((tok, columns), bf16),
        in_specs=[
            pl.BlockSpec(memory_space=pltpu.SMEM),
            pl.BlockSpec(memory_space=vmem),
            anywhere,
            anywhere,
            anywhere,
        ],
        out_specs=pl.BlockSpec(memory_space=vmem),
        scratch_shapes=[
            vmem((tok * heads, width), bf16),
            vmem(w_uv.shape, bf16),
            vmem((n_ctx * tok, width), bf16),
            vmem((LAT // 128, tok * heads, 128), f32),
            vmem((n_hi * VDIM, cols1), bf16),
            vmem((n_lo * VDIM, cols2), bf16),
            vmem((n_lo, tok, ratio * VDIM), bf16),
            vmem((ratio, tok, n_lo * VDIM), bf16),
            vmem((n_lo, n_head, tok, ratio * VDIM), bf16),
            vmem((n_hi, tok, n_lo * VDIM), bf16),
            vmem((n_lo, tok, cols1), f32),
            vmem((n_hi, tok, cols2), f32),
            vmem((n_lo, tok, cols1), bf16),
            vmem((n_hi, tok, cols2), bf16),
            vmem((n_lo, tok, cols1), bf16),
            vmem((n_hi, tok, cols2), bf16),
            dma((4,)),
            dma((n_hi,)),
            dma((n_hi,)),
            dma((n_hi, n_lo)),
            dma((n_hi, n_lo)),
            dma((n_hi, n_lo)),
            dma((n_hi, n_lo)),
            dma((2, n_hi)),
            dma((2, n_hi)),
            dma((2, n_lo)),
            dma((2, n_lo)),
            dma((n_lo, n_head)),
            dma((n_lo, n_head)),
            dma((ratio,)),
            dma((n_hi, n_head)),
            dma((n_hi,)),
            dma((len(chunks1), n_lo)),
            dma((len(chunks1), n_lo)),
            dma((len(chunks2), n_hi)),
            dma((len(chunks2), n_hi)),
        ],
        compiler_params=pltpu.CompilerParams(
            collective_id=0, has_side_effects=True, vmem_limit_bytes=56 * 1024 * 1024
        ),
    )(pair_perm, latent, queries.reshape(tok * heads, width), w_uv, w_out)


def solution(mesh):
    placed = (P("ctx", "head", None), P("ctx", None), P("head", None, None), P("ctx", "head"), P())
    return jax.shard_map(
        functools.partial(body, mesh.shape["ctx"], mesh.shape["head"]),
        mesh=mesh,
        in_specs=placed,
        out_specs=P("ctx", "head"),
        check_vma=False,
    )
```
